256 devices in a mesh: bin: 64 (over x, z, core), line: 4 (over y).
Axes of the slice: x: 4, y: 4, z: 8, core: 2. Of those that a mesh axis runs over, the one named last changes fastest.
Arguments:
- traces: float32 [4, 16384, 1024], P('line', 'bin'), may hold values from -6 to 6
- trace_cell: int32 [4, 16384], P('line', 'bin'), may hold values from 0 to 4095, as said below
- pattern: int32 [4, 16384], P('line', 'bin'), may hold values from 0 to 15
- fold: int32 [16, 1024], P('line', 'bin'), may hold values from 1 to 40, as said below
Outputs:
- spectrum: float32 [1024, 16, 1024], P('bin', 'line')
The draws below stay inside these ranges and needn't reach their ends.
Inputs may be any that keep to these rules, and one draw needn't show every extreme that they name: `trace_cell`: the traces held by one device lie in the bins of one index of bin at most 8 times, and that count is reached; the bins of each index of bin receive exactly 256 traces of each line group. fold[l, j] is the number of traces whose cell is (l, j); it reaches 40.
All inputs are finite; a program needn't handle non-finite values.
Results may differ from the reference program's by a relative error of at most 0.0001.
Values sent between devices are 32-bit elements; how exact they have to be, the bound alone decides.
A program may use at most 192 MiB of HBM per device.

```python
import math
import jax
import jax.numpy as jnp

NT = 1024
NF = 512
RADIUS = 2
PATTERNS = 16
FOLD = 40
LN_DEV = 4
BIN_DEV = 16
TR_DEV = 256
TR_GROUP = 16384
NL = 16
NB = 1024
N_BIN = 64
N_LINE = 4


def binning_layout(base_key):
    cells_dev = LN_DEV * BIN_DEV
    bins_line = BIN_DEV * N_BIN
    half_mean = TR_DEV // (2 * N_BIN)
    places = jnp.arange(TR_DEV, dtype=jnp.int32)
    remain = places - cells_dev - (FOLD - 1)
    indices = jnp.arange(1, cells_dev, dtype=jnp.int32)
    extra = jnp.minimum(FOLD - 6, cells_dev // 4 // indices)
    running = jnp.cumsum(extra)
    total_extra = running[-1]
    ranked = 1 + jnp.sum((running[None, :] <= remain[:, None]).astype(jnp.int32), axis=1)
    leftover = 1 + (remain - total_extra) % (cells_dev - 1)
    base = jnp.where(places < cells_dev, places, jnp.where(remain < 0, 0, jnp.where(remain < total_extra, ranked, leftover)))
    counts = jnp.sum((base[:, None] == jnp.arange(cells_dev, dtype=jnp.int32)[None, :]).astype(jnp.int32), axis=0)
    cell_groups = []
    fold_groups = []
    for group in range(N_LINE):
        subkeys = jax.random.split(jax.random.fold_in(base_key, group), 7)
        perm_one = jax.random.permutation(subkeys[0], N_BIN)
        perm_two = jax.random.permutation(subkeys[1], N_BIN)
        perm_three = jax.random.permutation(subkeys[2], N_BIN)
        perm_four = jax.random.permutation(subkeys[3], N_BIN)
        sign_first = 1 - 2 * ((perm_one[:, None] + perm_two[None, :]) % 2)
        sign_second = 1 - 2 * ((perm_three[:, None] + perm_four[None, :]) % 2)
        sends = 2 * half_mean + half_mean * sign_first + half_mean * sign_second
        cell_perm = jax.vmap(lambda single: jax.random.permutation(single, cells_dev))(jax.random.split(subkeys[4], N_BIN))
        labels = jnp.take_along_axis(cell_perm, jnp.broadcast_to(base, (N_BIN, TR_DEV)), axis=1)
        inverse = jnp.argsort(cell_perm, axis=1)
        fold_dest = counts[inverse]
        shuffle = jax.vmap(lambda single: jax.random.permutation(single, TR_DEV))(jax.random.split(subkeys[5], N_BIN))
        labels = jnp.take_along_axis(labels, shuffle, axis=1)
        row_cum = jnp.cumsum(sends, axis=1)
        row_start = row_cum - sends
        col_start = jnp.cumsum(sends, axis=0) - sends
        target = jnp.sum((row_cum[:, None, :] <= places[None, :, None]).astype(jnp.int32), axis=2)
        within = places[None, :] - jnp.take_along_axis(row_start, target, axis=1)
        position = jnp.take_along_axis(col_start, target, axis=1) + within
        local_cell = labels[target, position]
        reorder = jax.vmap(lambda single: jax.random.permutation(single, TR_DEV))(jax.random.split(subkeys[6], N_BIN))
        local_cell = jnp.take_along_axis(local_cell, reorder, axis=1)
        target = jnp.take_along_axis(target, reorder, axis=1)
        global_cell = local_cell // BIN_DEV * bins_line + target * BIN_DEV + local_cell % BIN_DEV
        cell_groups.append(global_cell.reshape(TR_DEV * N_BIN).astype(jnp.int32))
        fold_groups.append(jnp.transpose(fold_dest.reshape(N_BIN, LN_DEV, BIN_DEV), (1, 0, 2)).reshape(LN_DEV, bins_line).astype(jnp.int32))
    return (jnp.stack(cell_groups, axis=0), jnp.concatenate(fold_groups, axis=0))


def draw_trace_cell(key, part):
    return binning_layout(jax.random.fold_in(key, 7))[0]


def draw_fold(key, part):
    return binning_layout(jax.random.fold_in(key, 7))[1]


def touch_ends(values, stream_key, smallest, high):
    index_at = [jax.random.randint(jax.random.fold_in(stream_key, axis), (), 0, length) for axis, length in enumerate(values.shape)]
    main_axis = values.shape.index(max(values.shape))
    beside = index_at[:main_axis] + [(index_at[main_axis] + 1) % values.shape[main_axis]] + index_at[main_axis + 1:]
    return values.at[tuple(index_at)].set(smallest).at[tuple(beside)].set(high)


def block_levels(key, dims, cuts, least, high):
    def one(axis_at, shards_of):
        steps = jax.random.uniform(jax.random.fold_in(jax.random.fold_in(key, 6), axis_at), (shards_of,), jnp.float32, least / len(cuts), high / len(cuts))
        return jnp.repeat(jnp.exp(steps), dims[axis_at] // shards_of).reshape((-1,) + (1,) * (len(dims) - axis_at - 1))

    gain = one(*cuts[0])
    for cut in cuts[1:]:
        gain = gain * one(*cut)
    return gain


def normal_values(own_key, extent, scale, limit, cuts=(), held_as=jnp.bfloat16):
    values = jax.random.normal(own_key, extent, jnp.float32) * scale
    if len(cuts) > 0:
        values = block_levels(own_key, extent, cuts, -0.22, 0.18) * values
    return jnp.clip(values, min=-limit, max=limit).astype(held_as)


def setup_inputs(seed: int = 0) -> dict:
    streams_of = jax.random.split(jax.random.key(seed), 5)
    return {
        "traces": normal_values(streams_of[0], (N_LINE, TR_GROUP, NT), 1.0, 6.0, ((0, 4), (1, 64)), jnp.float32),
        "trace_cell": draw_trace_cell(jax.random.fold_in(streams_of[4], 71), 0),
        "pattern": touch_ends(jax.random.randint(streams_of[2], (N_LINE, TR_GROUP), 0, PATTERNS), jax.random.fold_in(streams_of[2], 1), 0, PATTERNS - 1).astype(jnp.int32),
        "fold": draw_fold(jax.random.fold_in(streams_of[4], 71), 0),
    }


def sinc_table():
    shifts = jnp.arange(-RADIUS, RADIUS + 1).astype(jnp.float32)
    offsets = (jnp.arange(PATTERNS).astype(jnp.float32) + 0.5) / PATTERNS - 0.5
    spread = shifts[:, None] - offsets[None, :]
    return jnp.sinc(spread) * jnp.cos(jnp.pi * spread / (2 * RADIUS + 2)) ** 2

def reference(traces, trace_cell, pattern, fold):
    sinc_weights = sinc_table()
    padded = jnp.zeros((NL + 2 * RADIUS, NB, NT), jnp.float32)
    for group in range(N_LINE):
        for offset in range(2 * RADIUS + 1):
            factor = sinc_weights[offset][pattern[group]]
            partial_value = jax.ops.segment_sum(factor[:, None] * traces[group], trace_cell[group], num_segments=LN_DEV * NB)
            partial_value = partial_value.reshape(LN_DEV, NB, NT)
            start_line = group * LN_DEV + offset
            padded = padded.at[start_line:start_line + LN_DEV].add(partial_value)
    regular = padded[RADIUS:RADIUS + NL] / fold.astype(jnp.float32)[:, :, None]
    transform = jnp.fft.rfft(regular, axis=-1)[..., :NF]
    scale = 1.0 / math.sqrt(NT)
    joined = jnp.concatenate([jnp.real(transform), jnp.imag(transform)], axis=-1) * scale
    return jnp.transpose(joined, (2, 0, 1)).astype(jnp.float32)
```

```python
import functools
import math

import jax
import jax.numpy as jnp
import numpy as np
from jax import lax
from jax.experimental import pallas as pl
from jax.experimental.pallas import tpu as pltpu
from jax.sharding import PartitionSpec as P

RADIUS = 2
PATTERNS = 16
NX, NZ, NC, NY = 4, 8, 2, 4
N_BIN = NX * NZ * NC
LANES = 128
GROUP = 4
NT_DOT = (((1,), (1,)), ((), ()))
MESH = pl.DeviceIdType.MESH


def sinc_table():
    shifts = np.arange(-RADIUS, RADIUS + 1)
    offsets = (np.arange(PATTERNS) + 0.5) / PATTERNS - 0.5
    spread = shifts[:, None] - offsets[None, :]
    table = np.zeros((8, LANES), np.float32)
    table[: 2 * RADIUS + 1, :PATTERNS] = (
        np.sinc(spread) * np.cos(np.pi * spread / (2 * RADIUS + 2)) ** 2
    )
    return table


def dft_tables(length):
    times = np.arange(length)
    freqs = np.arange(length // 2)
    phase = 2.0 * np.pi * (freqs[:, None] * times[None, :] % length) / length
    full = np.concatenate([np.cos(phase), -np.sin(phase)], axis=0) / math.sqrt(length)
    high = full.astype(jnp.bfloat16)
    low = (full - high.astype(np.float64)).astype(jnp.bfloat16)
    return high, low


def split(values):
    high = values.astype(jnp.bfloat16)
    return high, (values - high.astype(jnp.float32)).astype(jnp.bfloat16)


def dot_nt(a, b):
    return lax.dot_general(a, b, NT_DOT, preferred_element_type=jnp.float32)


def place():
    b = lax.axis_index("bin")
    return b // (NZ * NC), b // NC % NZ, b % NC, lax.axis_index("line")


def device(x, z, c):
    return (x * NZ + z) * NC + c


def kernel(
    traces_hbm, cell_ref, pattern_ref, fold_ref, high_hbm, low_hbm, sinc_ref,
    out_ref,
    traces, high, low, spec, recv, meta, folds, fold_sum, acc, onehot, mixed, halo,
    load_sem, meta_ssem, meta_rsem, fold_ssem, fold_rsem, send_sem, recv_sem, halo_ssem, halo_rsem,
):
    bins = acc.shape[1]
    x, z, c, y = place()
    me = device(x, z, c)

    def along_z(k):
        return device(x, (z + k) % NZ, c)

    def across(k):
        return device((x + k // NC) % NX, z, (c + k) % NC)

    loads = [
        pltpu.make_async_copy(src, dst, load_sem.at[i])
        for i, (src, dst) in enumerate(((traces_hbm, traces), (high_hbm, high), (low_hbm, low)))
    ]
    for load in loads:
        load.start()

    barrier = pltpu.get_barrier_semaphore()
    for k in range(1, NZ):
        pl.semaphore_signal(barrier, inc=1, device_id=(along_z(k), y), device_id_type=MESH)
    for k in range(1, NX * NC):
        pl.semaphore_signal(barrier, inc=1, device_id=(across(k), y), device_id_type=MESH)
    above, below = (y + 1) % NY, (y + NY - 1) % NY
    for other in (above, below):
        pl.semaphore_signal(barrier, inc=1, device_id=(me, other), device_id_type=MESH)

    for i in range(2):
        meta[0, 0, pl.ds(i, 1), :] = cell_ref[:, pl.ds(i * LANES, LANES)]
        meta[0, 0, pl.ds(2 + i, 1), :] = pattern_ref[:, pl.ds(i * LANES, LANES)]
    lanes = fold_ref.shape[1]
    spread_row = lax.broadcasted_iota(jnp.int32, (lanes, LANES), 0)
    spread_lane = lax.broadcasted_iota(jnp.int32, (lanes, LANES), 1)
    spread = (spread_lane == (z % 4) * (NC * lanes) + c * lanes + spread_row).astype(jnp.float32)
    fold_row = jnp.dot(
        fold_ref[...].astype(jnp.float32), spread, preferred_element_type=jnp.float32
    )
    fold_both = jnp.concatenate([fold_row, fold_row], axis=0)
    half = lax.broadcasted_iota(jnp.int32, fold_both.shape, 0) // 4
    folds[0] = jnp.where(half == z // 4, fold_both, 0.0)

    for load in loads:
        load.wait()
    t_high, t_low = split(traces[...])

    def transform(i, carry):
        rows = pl.ds(pl.multiple_of(i * 256, 256), 256)
        f_high = high[rows, :]
        spec[rows, :] = (
            dot_nt(f_high, t_low) + dot_nt(low[rows, :], t_high) + dot_nt(f_high, t_high)
        )
        return carry

    lax.fori_loop(0, spec.shape[0] // 256, transform, 0)

    pl.semaphore_wait(barrier, NZ - 1 + NX * NC - 1 + 2)

    first = []
    for k in range(1, NZ):
        first.append(pltpu.make_async_remote_copy(
            meta.at[0, 0], meta.at[0, k], meta_ssem.at[k], meta_rsem.at[k],
            device_id=(along_z(k), y), device_id_type=MESH))
        first.append(pltpu.make_async_remote_copy(
            folds.at[0], folds.at[k], fold_ssem.at[k], fold_rsem.at[k],
            device_id=(along_z(k), y), device_id_type=MESH))
    for copy in first:
        copy.start()
    for copy in first:
        copy.wait_recv()
    fold_sum[0] = jnp.sum(folds[...], axis=0)
    second = []
    for k in range(1, NX * NC):
        second.append(pltpu.make_async_remote_copy(
            meta.at[0], meta.at[k], meta_ssem.at[NZ + k], meta_rsem.at[NZ + k],
            device_id=(across(k), y), device_id_type=MESH))
        second.append(pltpu.make_async_remote_copy(
            fold_sum.at[0], fold_sum.at[k], fold_ssem.at[NZ + k], fold_rsem.at[NZ + k],
            device_id=(across(k), y), device_id_type=MESH))
    for copy in second:
        copy.start()
    for copy in second:
        copy.wait_recv()

    slice_rows = recv.shape[1]

    def sent(k):
        a, d = k // NZ, k % NZ
        target = device((x + a // NC) % NX, (z + d) % NZ, (c + a) % NC)
        return pltpu.make_async_remote_copy(
            spec.at[pl.ds(pl.multiple_of(target * slice_rows, slice_rows), slice_rows)],
            recv.at[k], send_sem.at[k], recv_sem.at[k],
            device_id=(target, y), device_id_type=MESH)

    def start_one(k, carry):
        sent(k).start()
        return carry

    lax.fori_loop(1, N_BIN, start_one, 0)
    recv[0] = spec[pl.ds(pl.multiple_of(me * slice_rows, slice_rows), slice_rows), :]

    acc[...] = jnp.zeros_like(acc)
    records = recv.shape[2]

    def stack(i, carry):
        for j in range(GROUP):
            k = i * GROUP + j

            @pl.when(k > 0)
            def _():
                sent(k).wait_recv()

            tags = meta[k // NZ, k % NZ]
            cell = jnp.concatenate([tags[0:1], tags[1:2]], axis=1)
            pattern = jnp.broadcast_to(
                jnp.concatenate([tags[2:3], tags[3:4]], axis=1), (8, records)
            )
            taps = jnp.zeros((8, records), jnp.float32)
            for q in range(PATTERNS):
                taps = jnp.where(pattern == q, sinc_ref[:, q : q + 1], taps)
            line = jnp.broadcast_to(cell // bins, (8, records))
            weights = taps
            for s in range(1, 4):
                weights = jnp.where(line == s, pltpu.roll(taps, s, 0), weights)
            terms = (weights[:, None, :] * recv[k][None, :, :]).reshape(8 * slice_rows, records)
            t_high, t_low = split(terms)
            columns = pl.ds(j * records, records)
            mixed[pl.ds(0, 8 * slice_rows), columns] = t_high
            mixed[pl.ds(8 * slice_rows, 8 * slice_rows), columns] = t_low
            where = cell % bins
            for g in range(0, bins, 256):
                row = lax.broadcasted_iota(jnp.int32, (256, records), 0) + g
                onehot[pl.ds(g, 256), columns] = (
                    (row == jnp.broadcast_to(where, (256, records)))
                    .astype(jnp.float32)
                    .astype(jnp.bfloat16)
                )
        for g in range(0, bins, 256):
            acc[:, pl.ds(g, 256)] += dot_nt(mixed[...], onehot[pl.ds(g, 256), :])
        return carry

    lax.fori_loop(0, N_BIN // GROUP, stack, 0)

    full = 8 * slice_rows
    edge = 2 * slice_rows
    halo[0] = acc[pl.ds(0, edge), :] + acc[pl.ds(full, edge), :]
    halo[1] = acc[pl.ds(full - edge, edge), :] + acc[pl.ds(2 * full - edge, edge), :]
    down = pltpu.make_async_remote_copy(
        halo.at[0], halo.at[2], halo_ssem.at[0], halo_rsem.at[0],
        device_id=(me, below), device_id_type=MESH)
    up = pltpu.make_async_remote_copy(
        halo.at[1], halo.at[3], halo_ssem.at[1], halo_rsem.at[1],
        device_id=(me, above), device_id_type=MESH)
    down.start()
    up.start()
    counts = []
    for i in range(NX):
        block = None
        for j in range(NC):
            slot = (x + NX - i) % NX * NC + j
            part = fold_sum[slot]
            block = part if block is None else block + part
        counts.append(block)
    inverse = 1.0 / jnp.concatenate(
        [block[4 * h : 4 * h + 4] for block in counts for h in range(2)], axis=1
    )
    down.wait()
    up.wait()
    for line in range(4):
        rows = pl.ds((line + 2) * slice_rows, slice_rows)
        low_rows = pl.ds(full + (line + 2) * slice_rows, slice_rows)
        value = acc[rows, :] + acc[low_rows, :]
        if line < 2:
            extra = halo[3, pl.ds(line * slice_rows, slice_rows), :]
            inside = y > 0
        else:
            extra = halo[2, pl.ds((line - 2) * slice_rows, slice_rows), :]
            inside = y < NY - 1
        value = value + jnp.where(inside, extra, 0.0)
        out_ref[:, line, :] = value * inverse[line : line + 1, :]

    for copy in first + second:
        copy.wait_send()

    def finish_one(k, carry):
        sent(k).wait_send()
        return carry

    lax.fori_loop(1, N_BIN, finish_one, 0)


def per_device(traces, trace_cell, pattern, fold):
    _, records, length = traces.shape
    lines, bins_dev = fold.shape
    bins = bins_dev * N_BIN
    rows = length // N_BIN
    high, low = dft_tables(length)
    anywhere = pl.BlockSpec(memory_space=pl.ANY)
    vmem = pl.BlockSpec(memory_space=pltpu.VMEM)
    f32, i32, bf16 = jnp.float32, jnp.int32, jnp.bfloat16
    return pl.pallas_call(
        kernel,
        out_shape=jax.ShapeDtypeStruct((rows, lines, bins), f32),
        in_specs=[anywhere, vmem, vmem, vmem, anywhere, anywhere, vmem],
        out_specs=vmem,
        scratch_shapes=[
            pltpu.VMEM((records, length), f32),
            pltpu.VMEM((length, length), bf16),
            pltpu.VMEM((length, length), bf16),
            pltpu.VMEM((length, records), f32),
            pltpu.VMEM((N_BIN, rows, records), f32),
            pltpu.VMEM((NX * NC, NZ, 4, LANES), i32),
            pltpu.VMEM((NZ, 8, LANES), f32),
            pltpu.VMEM((NX * NC, 8, LANES), f32),
            pltpu.VMEM((16 * rows, bins), f32),
            pltpu.VMEM((bins, GROUP * records), bf16),
            pltpu.VMEM((16 * rows, GROUP * records), bf16),
            pltpu.VMEM((4, 2 * rows, bins), f32),
            pltpu.SemaphoreType.DMA((3,)),
            pltpu.SemaphoreType.DMA((2 * NZ,)),
            pltpu.SemaphoreType.DMA((2 * NZ,)),
            pltpu.SemaphoreType.DMA((2 * NZ,)),
            pltpu.SemaphoreType.DMA((2 * NZ,)),
            pltpu.SemaphoreType.DMA((N_BIN,)),
            pltpu.SemaphoreType.DMA((N_BIN,)),
            pltpu.SemaphoreType.DMA((2,)),
            pltpu.SemaphoreType.DMA((2,)),
        ],
        compiler_params=pltpu.CompilerParams(
            collective_id=0, has_side_effects=True, vmem_limit_bytes=48 << 20
        ),
    )(traces[0], trace_cell, pattern, fold, jnp.asarray(high), jnp.asarray(low), jnp.asarray(sinc_table()))


def solution(mesh):
    return jax.shard_map(
        per_device,
        mesh=mesh,
        in_specs=(P("line", "bin", None), P("line", "bin"), P("line", "bin"), P("line", "bin")),
        out_specs=P("bin", "line", None),
        check_vma=False,
    )
```

```python
import functools
import math

import jax
import jax.numpy as jnp
import numpy as np
from jax import lax
from jax.experimental import pallas as pl
from jax.experimental.pallas import tpu as pltpu
from jax.sharding import PartitionSpec as P

RADIUS = 2
PATTERNS = 16
NX, NZ, NC, NY = 4, 8, 2, 4
N_BIN = NX * NZ * NC
LANES = 128
GROUP = 4
NT_DOT = (((1,), (1,)), ((), ()))
MESH = pl.DeviceIdType.MESH


def sinc_table():
    shifts = np.arange(-RADIUS, RADIUS + 1)
    offsets = (np.arange(PATTERNS) + 0.5) / PATTERNS - 0.5
    spread = shifts[:, None] - offsets[None, :]
    table = np.zeros((8, LANES), np.float32)
    table[: 2 * RADIUS + 1, :PATTERNS] = (
        np.sinc(spread) * np.cos(np.pi * spread / (2 * RADIUS + 2)) ** 2
    )
    return table


def dft_table(length):
    times = np.arange(length // 2)
    freqs = np.arange(length // 2)
    phase = 2.0 * np.pi * (freqs[:, None] * times[None, :] % length) / length
    full = np.concatenate([np.cos(phase), -np.sin(phase)], axis=0) / math.sqrt(length)
    full = full.reshape(NX, -1, 2, length // 2).transpose(0, 2, 1, 3)
    high = full.astype(jnp.bfloat16)
    low = (full - high.astype(np.float64)).astype(jnp.bfloat16)
    return np.concatenate([high, low], axis=2)


def split(values):
    high = values.astype(jnp.bfloat16)
    return high, (values - high.astype(jnp.float32)).astype(jnp.bfloat16)


def dot_nt(a, b):
    return lax.dot_general(a, b, NT_DOT, preferred_element_type=jnp.float32)


def place():
    b = lax.axis_index("bin")
    return b // (NZ * NC), b // NC % NZ, b % NC, lax.axis_index("line")


def device(x, z, c):
    return (x * NZ + z) * NC + c


def kernel(
    traces_hbm, cell_hbm, pattern_hbm, fold_hbm, table_hbm, sinc_hbm,
    out_ref,
    traces, cells, patterns, own_fold, table, sinc, spec, recv, meta, folds, fold_sum, acc, onehot, mixed, halo,
    load_sem, entered, meta_ssem, meta_rsem, fold_ssem, fold_rsem, send_sem, recv_sem, halo_ssem, halo_rsem,
):
    bins = acc.shape[1]
    x, z, c, y = place()
    me = device(x, z, c)
    above, below = (y + 1) % NY, (y + NY - 1) % NY
    columns = NX * NC

    def along_z(k):
        return device(x, (z + k) % NZ, c), y

    def across(k):
        return device((x + k // NC) % NX, z, (c + k) % NC), y

    barrier = pltpu.get_barrier_semaphore()
    neighbours = [along_z(k) for k in range(1, NZ)] + [across(k) for k in range(1, columns)]
    neighbours += [(me, above), (me, below)]
    for other in neighbours:
        pl.semaphore_signal(barrier, inc=1, device_id=other, device_id_type=MESH)

    pairs = [(cell_hbm, cells), (pattern_hbm, patterns), (traces_hbm, traces)]
    pairs += [(table_hbm.at[(x + i) % NX], table.at[i]) for i in range(NX)]
    pairs += [(fold_hbm, own_fold), (sinc_hbm, sinc)]
    loads = [
        pltpu.make_async_copy(source, target, load_sem.at[i])
        for i, (source, target) in enumerate(pairs)
    ]
    for load in loads:
        load.start()

    loads[0].wait()
    loads[1].wait()
    for i in range(2):
        meta[0, 0, pl.ds(i, 1), :] = cells[:, pl.ds(i * LANES, LANES)]
        meta[0, 0, pl.ds(2 + i, 1), :] = patterns[:, pl.ds(i * LANES, LANES)]

    pl.semaphore_wait(barrier, len(neighbours))
    for k in range(1, columns):
        pl.semaphore_signal(entered, inc=1, device_id=across(k), device_id_type=MESH)
    meta_along = [
        pltpu.make_async_remote_copy(
            meta.at[0, 0], meta.at[0, k], meta_ssem.at[k], meta_rsem.at[k],
            device_id=along_z(k), device_id_type=MESH)
        for k in range(1, NZ)
    ]
    for copy in meta_along:
        copy.start()

    loads[2].wait()
    middle = traces.shape[1] // 2
    early, late = traces[:, :middle], traces[:, middle:]
    parts = [split(early + late), split(early - late)]

    def transform(i):
        loads[3 + i].wait()
        for parity, (t_high, t_low) in enumerate(parts):
            both = dot_nt(table[i, parity], t_high)
            rows = both.shape[0] // 2
            value = both[:rows] + both[rows:] + dot_nt(table[i, parity, :rows], t_low)
            at = pl.ds((x + i) % NX * (NZ * NC), NZ * NC)
            spec[at, parity] = value.reshape(NZ * NC, rows // (NZ * NC), -1)

    def sent(k):
        a, d = k // NZ, k % NZ
        target = device((x + a // NC) % NX, (z + d) % NZ, (c + a) % NC)
        return pltpu.make_async_remote_copy(
            spec.at[target], recv.at[k], send_sem.at[k], recv_sem.at[k],
            device_id=(target, y), device_id_type=MESH)

    def start_one(k, carry):
        sent(k).start()
        return carry

    transform(0)
    lax.fori_loop(1, NZ, start_one, 0)
    pl.semaphore_wait(entered, columns - 1)
    lax.fori_loop(NZ, NZ * NC, start_one, 0)
    for copy in meta_along:
        copy.wait_recv()
    meta_across = [
        pltpu.make_async_remote_copy(
            meta.at[0], meta.at[k], meta_ssem.at[NZ + k], meta_rsem.at[NZ + k],
            device_id=across(k), device_id_type=MESH)
        for k in range(1, columns)
    ]
    for copy in meta_across:
        copy.start()
    for i in range(1, NX):
        transform(i)
        lax.fori_loop(NZ * NC * i, NZ * NC * (i + 1), start_one, 0)
    recv[0] = spec[me]

    loads[-1].wait()
    loads[-2].wait()
    lanes = own_fold.shape[1]
    spread_row = lax.broadcasted_iota(jnp.int32, (lanes, LANES), 0)
    spread_lane = lax.broadcasted_iota(jnp.int32, (lanes, LANES), 1)
    spread = (spread_lane == (z % 4) * (NC * lanes) + c * lanes + spread_row).astype(jnp.float32)
    fold_row = jnp.dot(
        own_fold[...].astype(jnp.float32), spread, preferred_element_type=jnp.float32
    )
    fold_both = jnp.concatenate([fold_row, fold_row], axis=0)
    half = lax.broadcasted_iota(jnp.int32, fold_both.shape, 0) // 4
    folds[0] = jnp.where(half == z // 4, fold_both, 0.0)
    fold_along = [
        pltpu.make_async_remote_copy(
            folds.at[0], folds.at[k], fold_ssem.at[k], fold_rsem.at[k],
            device_id=along_z(k), device_id_type=MESH)
        for k in range(1, NZ)
    ]
    for copy in fold_along:
        copy.start()
    acc[...] = jnp.zeros_like(acc)
    for copy in meta_across:
        copy.wait_recv()
    for copy in fold_along:
        copy.wait_recv()
    fold_sum[0] = jnp.sum(folds[...], axis=0)
    fold_across = [
        pltpu.make_async_remote_copy(
            fold_sum.at[0], fold_sum.at[k], fold_ssem.at[NZ + k], fold_rsem.at[NZ + k],
            device_id=across(k), device_id_type=MESH)
        for k in range(1, columns)
    ]
    for copy in fold_across:
        copy.start()

    slice_rows = recv.shape[1] * recv.shape[2]
    records = recv.shape[3]
    full = 8 * slice_rows

    def stack(i, carry):
        weights = []
        for j in range(GROUP):
            k = i * GROUP + j
            tags = meta[k // NZ, k % NZ]
            cell = jnp.concatenate([tags[0:1], tags[1:2]], axis=1)
            pattern = jnp.broadcast_to(
                jnp.concatenate([tags[2:3], tags[3:4]], axis=1), (8, records)
            )
            taps = jnp.zeros((8, records), jnp.float32)
            for q in range(PATTERNS):
                taps = jnp.where(pattern == q, sinc[:, q : q + 1], taps)
            line = jnp.broadcast_to(cell // bins, (8, records))
            shifted = taps
            for s in range(1, 4):
                shifted = jnp.where(line == s, pltpu.roll(taps, s, 0), shifted)
            weights.append(shifted)
            where = cell % bins
            for g in range(0, bins, 256):
                row = lax.broadcasted_iota(jnp.int32, (256, records), 0) + g
                onehot[pl.ds(g, 256), pl.ds(j * records, records)] = (
                    (row == jnp.broadcast_to(where, (256, records)))
                    .astype(jnp.float32)
                    .astype(jnp.bfloat16)
                )
        for j in range(GROUP):
            k = i * GROUP + j

            @pl.when(k > 0)
            def _():
                sent(k).wait_recv()

            block = recv[k].reshape(slice_rows, records)
            terms = (weights[j][:, None, :] * block[None, :, :]).reshape(full, records)
            t_high, t_low = split(terms)
            mixed[pl.ds(0, full), pl.ds(j * records, records)] = t_high
            mixed[pl.ds(full, full), pl.ds(j * records, records)] = t_low
        for g in range(0, bins, 256):
            acc[:, pl.ds(g, 256)] += dot_nt(mixed[...], onehot[pl.ds(g, 256), :])
        return carry

    lax.fori_loop(0, N_BIN // GROUP, stack, 0)

    edge = 2 * slice_rows
    halo[0] = acc[pl.ds(0, edge), :] + acc[pl.ds(full, edge), :]
    halo[1] = acc[pl.ds(full - edge, edge), :] + acc[pl.ds(2 * full - edge, edge), :]
    down = pltpu.make_async_remote_copy(
        halo.at[0], halo.at[2], halo_ssem.at[0], halo_rsem.at[0],
        device_id=(me, below), device_id_type=MESH)
    up = pltpu.make_async_remote_copy(
        halo.at[1], halo.at[3], halo_ssem.at[1], halo_rsem.at[1],
        device_id=(me, above), device_id_type=MESH)
    down.start()
    up.start()
    for copy in fold_across:
        copy.wait_recv()
    counts = []
    for i in range(NX):
        slot = (x + NX - i) % NX * NC
        counts.append(fold_sum[slot] + fold_sum[slot + 1])
    inverse = 1.0 / jnp.concatenate(
        [block[4 * h : 4 * h + 4] for block in counts for h in range(2)], axis=1
    )

    def finish_one(k, carry):
        sent(k).wait_send()
        return carry

    lax.fori_loop(1, N_BIN, finish_one, 0)
    for copy in meta_along + meta_across + fold_along + fold_across:
        copy.wait_send()
    down.wait()
    up.wait()
    for line in range(4):
        value = acc[pl.ds((line + 2) * slice_rows, slice_rows), :]
        value = value + acc[pl.ds(full + (line + 2) * slice_rows, slice_rows), :]
        if line < 2:
            extra = halo[3, pl.ds(line * slice_rows, slice_rows), :]
            inside = y > 0
        else:
            extra = halo[2, pl.ds((line - 2) * slice_rows, slice_rows), :]
            inside = y < NY - 1
        value = (value + jnp.where(inside, extra, 0.0)) * inverse[line : line + 1, :]
        for parity in range(2):
            out_ref[:, parity, line, :] = value[parity * 8 : parity * 8 + 8]


def per_device(traces, trace_cell, pattern, fold):
    _, records, length = traces.shape
    lines, bins_dev = fold.shape
    bins = bins_dev * N_BIN
    rows = length // N_BIN
    table = dft_table(length)
    anywhere = pl.BlockSpec(memory_space=pl.ANY)
    f32, i32, bf16 = jnp.float32, jnp.int32, jnp.bfloat16
    dma = pltpu.SemaphoreType.DMA
    out = pl.pallas_call(
        kernel,
        out_shape=jax.ShapeDtypeStruct((rows // 2, 2, lines, bins), f32),
        in_specs=[anywhere] * 6,
        out_specs=pl.BlockSpec(memory_space=pltpu.VMEM),
        scratch_shapes=[
            pltpu.VMEM((records, length), f32),
            pltpu.VMEM((1, records), i32),
            pltpu.VMEM((1, records), i32),
            pltpu.VMEM((lines, bins_dev), i32),
            pltpu.VMEM(table.shape, bf16),
            pltpu.VMEM((8, LANES), f32),
            pltpu.VMEM((N_BIN, 2, rows // 2, records), f32),
            pltpu.VMEM((N_BIN, 2, rows // 2, records), f32),
            pltpu.VMEM((NX * NC, NZ, 4, LANES), i32),
            pltpu.VMEM((NZ, 8, LANES), f32),
            pltpu.VMEM((NX * NC, 8, LANES), f32),
            pltpu.VMEM((16 * rows, bins), f32),
            pltpu.VMEM((bins, GROUP * records), bf16),
            pltpu.VMEM((16 * rows, GROUP * records), bf16),
            pltpu.VMEM((4, 2 * rows, bins), f32),
            dma((5 + NX,)),
            pltpu.SemaphoreType.REGULAR,
            dma((2 * NZ,)),
            dma((2 * NZ,)),
            dma((2 * NZ,)),
            dma((2 * NZ,)),
            dma((N_BIN,)),
            dma((N_BIN,)),
            dma((2,)),
            dma((2,)),
        ],
        compiler_params=pltpu.CompilerParams(
            collective_id=0, has_side_effects=True, vmem_limit_bytes=63 << 20
        ),
    )(traces[0], trace_cell, pattern, fold, jnp.asarray(table), jnp.asarray(sinc_table()))
    return out.reshape(rows, lines, bins)


def solution(mesh):
    return jax.shard_map(
        per_device,
        mesh=mesh,
        in_specs=(P("line", "bin", None), P("line", "bin"), P("line", "bin"), P("line", "bin")),
        out_specs=P("bin", "line", None),
        check_vma=False,
    )
```

```python
import functools
import math

import jax
import jax.numpy as jnp
import numpy as np
from jax import lax
from jax.experimental import pallas as pl
from jax.experimental.pallas import tpu as pltpu
from jax.sharding import PartitionSpec as P

RADIUS = 2
PATTERNS = 16
NX, NZ, NC, NY = 4, 8, 2, 4
N_BIN = NX * NZ * NC
LANES = 128
GROUP = 8
LAST = 4
NT_DOT = (((1,), (1,)), ((), ()))
MESH = pl.DeviceIdType.MESH


def sinc_table():
    shifts = np.arange(-RADIUS, RADIUS + 1)
    offsets = (np.arange(PATTERNS) + 0.5) / PATTERNS - 0.5
    spread = shifts[:, None] - offsets[None, :]
    table = np.zeros((8, LANES), np.float32)
    table[: 2 * RADIUS + 1, :PATTERNS] = (
        np.sinc(spread) * np.cos(np.pi * spread / (2 * RADIUS + 2)) ** 2
    )
    return table


def dft_table(length):
    times = np.arange(length // 2)
    freqs = np.arange(length // 2)
    phase = 2.0 * np.pi * (freqs[:, None] * times[None, :] % length) / length
    full = np.concatenate([np.cos(phase), -np.sin(phase)], axis=0) / math.sqrt(length)
    full = full.reshape(NX, -1, 2, length // 2).transpose(0, 2, 1, 3)
    high = full.astype(jnp.bfloat16)
    low = (full - high.astype(np.float64)).astype(jnp.bfloat16)
    return np.concatenate([high, low], axis=2)


def split(values):
    high = values.astype(jnp.bfloat16)
    return high, (values - high.astype(jnp.float32)).astype(jnp.bfloat16)


def dot_nt(a, b):
    return lax.dot_general(a, b, NT_DOT, preferred_element_type=jnp.float32)


def place():
    b = lax.axis_index("bin")
    return b // (NZ * NC), b // NC % NZ, b % NC, lax.axis_index("line")


def device(x, z, c):
    return (x * NZ + z) * NC + c


X_ORDER = (0, 2, 1, 3)
OWN = NZ * NC - NC


def offsets(k):
    i, d, e = k // (NZ * NC), k // NC % NZ, k % NC
    along_x = jnp.where(i == 1, X_ORDER[1], jnp.where(i == 2, X_ORDER[2], i))
    along_z = NZ // 2 + jnp.where(d % 2 == 1, -((d + 1) // 2), d // 2)
    return along_x, along_z, e


def unit_of(k):
    late = k - (N_BIN - 2 * LAST)
    return jnp.where(late < 0, k // GROUP, (N_BIN - 2 * LAST) // GROUP + late // LAST)


def wait_for(ref, sem):
    pltpu.make_async_copy(ref, ref, sem).wait()


def kernel(
    traces_hbm, cell_hbm, pattern_hbm, fold_hbm, table_hbm, sinc_hbm,
    out_ref,
    traces, cells, patterns, own_fold, table, sinc, spec, recv, meta, folds, fold_sum, acc, onehot, mixed, halo,
    load_sem, entered, meta_sem, fold_sem, send_sem, recv_sem, halo_sem,
):
    bins = acc.shape[1]
    x, z, c, y = place()
    me = device(x, z, c)
    above, below = (y + 1) % NY, (y + NY - 1) % NY
    columns = NX * NC

    def along_z(k):
        return device(x, (z + k) % NZ, c), y

    def across(k):
        return device((x + k // NC) % NX, z, (c + k) % NC), y

    def copies(ref, slots, peer, sem):
        for k in range(1, slots):
            pltpu.make_async_remote_copy(
                ref.at[0], ref.at[k], sem.at[0], sem.at[1],
                device_id=peer(k), device_id_type=MESH).start()

    barrier = pltpu.get_barrier_semaphore()
    neighbours = [along_z(k) for k in range(1, NZ)] + [across(k) for k in range(1, columns)]
    neighbours += [(me, above), (me, below)]
    for other in neighbours:
        pl.semaphore_signal(barrier, inc=1, device_id=other, device_id_type=MESH)

    pairs = [(cell_hbm, cells), (pattern_hbm, patterns), (fold_hbm, own_fold), (traces_hbm, traces)]
    pairs += [(table_hbm.at[(x + i) % NX], table.at[n]) for n, i in enumerate(X_ORDER)]
    pairs += [(sinc_hbm, sinc)]
    loads = [
        pltpu.make_async_copy(source, target, load_sem.at[i])
        for i, (source, target) in enumerate(pairs)
    ]
    for load in loads:
        load.start()

    pl.semaphore_wait(barrier, len(neighbours))
    for k in range(1, columns):
        pl.semaphore_signal(entered, inc=1, device_id=across(k), device_id_type=MESH)

    loads[0].wait()
    loads[1].wait()
    for i in range(2):
        meta[0, 0, pl.ds(i, 1), :] = cells[:, pl.ds(i * LANES, LANES)]
        meta[0, 0, pl.ds(2 + i, 1), :] = patterns[:, pl.ds(i * LANES, LANES)]
    copies(meta.at[0], NZ, along_z, meta_sem.at[0])
    loads[2].wait()
    lanes = own_fold.shape[1]
    spread_row = lax.broadcasted_iota(jnp.int32, (lanes, LANES), 0)
    spread_lane = lax.broadcasted_iota(jnp.int32, (lanes, LANES), 1)
    spread = (spread_lane == (z % 4) * (NC * lanes) + c * lanes + spread_row).astype(jnp.float32)
    fold_row = jnp.dot(
        own_fold[...].astype(jnp.float32), spread, preferred_element_type=jnp.float32
    )
    fold_both = jnp.concatenate([fold_row, fold_row], axis=0)
    half = lax.broadcasted_iota(jnp.int32, fold_both.shape, 0) // 4
    folds[0] = jnp.where(half == z // 4, fold_both, 0.0)
    copies(folds, NZ, along_z, fold_sem.at[0])

    loads[3].wait()
    middle = traces.shape[1] // 2
    early, late = traces[:, :middle], traces[:, middle:]
    parts = [split(early + late), split(early - late)]

    def transform(i):
        loads[4 + i].wait()
        for parity, (t_high, t_low) in enumerate(parts):
            both = dot_nt(table[i, parity], t_high)
            rows = both.shape[0] // 2
            value = both[:rows] + both[rows:] + dot_nt(table[i, parity, :rows], t_low)
            at = pl.ds((x + X_ORDER[i]) % NX * (NZ * NC), NZ * NC)
            spec[at, parity] = value.reshape(NZ * NC, rows // (NZ * NC), -1)

    def start(k):
        i, d, e = offsets(k)
        target = device((x + i) % NX, (z + d) % NZ, (c + e) % NC)
        pltpu.make_async_remote_copy(
            spec.at[target], recv.at[k], send_sem.at[0], recv_sem.at[unit_of(k)],
            device_id=(target, y), device_id_type=MESH).start()

    def start_one(k, carry):
        start(k)
        return carry

    transform(0)
    for d in range(NZ - 1):
        start(d * NC)
    pltpu.make_async_copy(spec.at[me], recv.at[OWN], recv_sem.at[unit_of(OWN)]).start()
    pl.semaphore_wait(entered, columns - 1)
    for d in range(NZ):
        start(d * NC + 1)
    wait_for(meta.at[0, pl.ds(1, NZ - 1)], meta_sem.at[0, 1])
    copies(meta, columns, across, meta_sem.at[1])
    wait_for(folds.at[pl.ds(1, NZ - 1)], fold_sem.at[0, 1])
    fold_sum[0] = jnp.sum(folds[...], axis=0)
    copies(fold_sum, columns, across, fold_sem.at[1])
    for i in range(1, NX):
        transform(i)
        lax.fori_loop(i * NZ * NC, (i + 1) * NZ * NC, start_one, 0)

    loads[-1].wait()
    acc[...] = jnp.zeros_like(acc)
    wait_for(meta.at[pl.ds(1, columns - 1)], meta_sem.at[1, 1])

    slice_rows = recv.shape[1] * recv.shape[2]
    records = recv.shape[3]
    full = 8 * slice_rows

    def tags_of(k):
        i, d, e = offsets(k)
        tags = meta[i * NC + e, d]
        return (
            jnp.concatenate([tags[0:1], tags[1:2]], axis=1),
            jnp.concatenate([tags[2:3], tags[3:4]], axis=1),
        )

    def weigh(cell, pattern):
        pattern = jnp.broadcast_to(pattern, (8, records))
        taps = jnp.zeros((8, records), jnp.float32)
        for q in range(PATTERNS):
            taps = jnp.where(pattern == q, sinc[:, q : q + 1], taps)
        line = jnp.broadcast_to(cell // bins, (8, records))
        weights = taps
        for s in range(1, 4):
            weights = jnp.where(line == s, pltpu.roll(taps, s, 0), weights)
        return jnp.concatenate([weights[0:2], weights[6:8], weights[2:6]], axis=0)

    def mark(j, cell):
        where = cell % bins
        for g in range(0, bins, 256):
            row = lax.broadcasted_iota(jnp.int32, (256, records), 0) + g
            onehot[pl.ds(g, 256), pl.ds(j * records, records)] = (
                (row == jnp.broadcast_to(where, (256, records)))
                .astype(jnp.float32)
                .astype(jnp.bfloat16)
            )

    def mix(k, j, weights):
        block = recv[k].reshape(slice_rows, records)
        terms = (weights[:, None, :] * block[None, :, :]).reshape(full, records)
        t_high, t_low = split(terms)
        at = pl.ds(j * records, records)
        edge = full // 2
        mixed[pl.ds(0, edge), at] = t_high[:edge]
        mixed[pl.ds(edge, edge), at] = t_low[:edge]
        mixed[pl.ds(2 * edge, edge), at] = t_high[edge:]
        mixed[pl.ds(3 * edge, edge), at] = t_low[edge:]

    def add(rows, count):
        depth = pl.ds(0, count * records)
        for g in range(0, bins, 256):
            acc[rows, pl.ds(g, 256)] += dot_nt(mixed[rows, depth], onehot[pl.ds(g, 256), depth])

    def stack(i, carry):
        wait_for(recv.at[pl.ds(i * GROUP, GROUP)], recv_sem.at[i])
        for j in range(GROUP):
            k = i * GROUP + j
            cell, pattern = tags_of(k)
            mix(k, j, weigh(cell, pattern))
            mark(j, cell)
        add(pl.ds(0, 2 * full), GROUP)
        return carry

    whole = (N_BIN - 2 * LAST) // GROUP
    lax.fori_loop(0, whole, stack, 0)

    def prepare(at):
        weights = []
        for j in range(LAST):
            cell, pattern = tags_of(at + j)
            weights.append(weigh(cell, pattern))
            mark(j, cell)
        return weights

    weights = prepare(N_BIN - 2 * LAST)
    wait_for(recv.at[pl.ds(N_BIN - 2 * LAST, LAST)], recv_sem.at[whole])
    for j in range(LAST):
        mix(N_BIN - 2 * LAST + j, j, weights[j])
    add(pl.ds(0, 2 * full), LAST)
    weights = prepare(N_BIN - LAST)
    wait_for(fold_sum.at[pl.ds(1, columns - 1)], fold_sem.at[1, 1])
    counts = []
    for i in range(NX):
        slot = (x + NX - i) % NX * NC
        counts.append(fold_sum[slot] + fold_sum[slot + 1])
    inverse = 1.0 / jnp.concatenate(
        [block[4 * h : 4 * h + 4] for block in counts for h in range(2)], axis=1
    )
    wait_for(recv.at[pl.ds(N_BIN - LAST, LAST)], recv_sem.at[whole + 1])
    for j in range(LAST):
        mix(N_BIN - LAST + j, j, weights[j])
    add(pl.ds(0, full), LAST)
    edge = 2 * slice_rows
    for i in range(2):
        halo[i] = acc[pl.ds(i * edge, edge), :] + acc[pl.ds((2 + i) * edge, edge), :]
    swaps = [
        pltpu.make_async_remote_copy(
            halo.at[i], halo.at[2 + i], halo_sem.at[0, i], halo_sem.at[1, i],
            device_id=(me, other), device_id_type=MESH)
        for i, other in enumerate((below, above))
    ]
    for swap in swaps:
        swap.start()
    add(pl.ds(full, full), LAST)
    wait_for(meta.at[0, pl.ds(1, NZ - 1)], meta_sem.at[0, 0])
    wait_for(meta.at[pl.ds(1, columns - 1)], meta_sem.at[1, 0])
    wait_for(folds.at[pl.ds(1, NZ - 1)], fold_sem.at[0, 0])
    wait_for(fold_sum.at[pl.ds(1, columns - 1)], fold_sem.at[1, 0])
    wait_for(recv.at[pl.ds(1, N_BIN - 1)], send_sem.at[0])
    for swap in swaps:
        swap.wait()
    for line in range(4):
        at = full + line * slice_rows
        value = acc[pl.ds(at, slice_rows), :] + acc[pl.ds(at + full // 2, slice_rows), :]
        if line < 2:
            extra = halo[3, pl.ds(line * slice_rows, slice_rows), :]
            inside = y > 0
        else:
            extra = halo[2, pl.ds((line - 2) * slice_rows, slice_rows), :]
            inside = y < NY - 1
        value = (value + jnp.where(inside, extra, 0.0)) * inverse[line : line + 1, :]
        for parity in range(2):
            out_ref[:, parity, line, :] = value[parity * 8 : parity * 8 + 8]


def per_device(traces, trace_cell, pattern, fold):
    _, records, length = traces.shape
    lines, bins_dev = fold.shape
    bins = bins_dev * N_BIN
    rows = length // N_BIN
    table = dft_table(length)
    anywhere = pl.BlockSpec(memory_space=pl.ANY)
    f32, i32, bf16 = jnp.float32, jnp.int32, jnp.bfloat16
    dma = pltpu.SemaphoreType.DMA
    out = pl.pallas_call(
        kernel,
        out_shape=jax.ShapeDtypeStruct((rows // 2, 2, lines, bins), f32),
        in_specs=[anywhere] * 6,
        out_specs=pl.BlockSpec(memory_space=pltpu.VMEM),
        scratch_shapes=[
            pltpu.VMEM((records, length), f32),
            pltpu.VMEM((1, records), i32),
            pltpu.VMEM((1, records), i32),
            pltpu.VMEM((lines, bins_dev), i32),
            pltpu.VMEM(table.shape, bf16),
            pltpu.VMEM((8, LANES), f32),
            pltpu.VMEM((N_BIN, 2, rows // 2, records), f32),
            pltpu.VMEM((N_BIN, 2, rows // 2, records), f32),
            pltpu.VMEM((NX * NC, NZ, 4, LANES), i32),
            pltpu.VMEM((NZ, 8, LANES), f32),
            pltpu.VMEM((NX * NC, 8, LANES), f32),
            pltpu.VMEM((16 * rows, bins), f32),
            pltpu.VMEM((bins, GROUP * records), bf16),
            pltpu.VMEM((16 * rows, GROUP * records), bf16),
            pltpu.VMEM((4, 2 * rows, bins), f32),
            dma((5 + NX,)),
            pltpu.SemaphoreType.REGULAR,
            dma((2, 2)),
            dma((2, 2)),
            dma((1,)),
            dma((N_BIN // GROUP + 1,)),
            dma((2, 2)),
        ],
        compiler_params=pltpu.CompilerParams(
            collective_id=0, has_side_effects=True, vmem_limit_bytes=63 << 20
        ),
    )(traces[0], trace_cell, pattern, fold, jnp.asarray(table), jnp.asarray(sinc_table()))
    return out.reshape(rows, lines, bins)


def solution(mesh):
    return jax.shard_map(
        per_device,
        mesh=mesh,
        in_specs=(P("line", "bin", None), P("line", "bin"), P("line", "bin"), P("line", "bin")),
        out_specs=P("bin", "line", None),
        check_vma=False,
    )
```

```python
import functools
import math

import jax
import jax.numpy as jnp
import numpy as np
from jax import lax
from jax.experimental import pallas as pl
from jax.experimental.pallas import tpu as pltpu
from jax.sharding import PartitionSpec as P

RADIUS = 2
PATTERNS = 16
NX, NZ, NC, NY = 4, 8, 2, 4
N_BIN = NX * NZ * NC
LANES = 128
GROUP = 8
LAST = 4
NT_DOT = (((1,), (1,)), ((), ()))
MESH = pl.DeviceIdType.MESH


def sinc_table():
    shifts = np.arange(-RADIUS, RADIUS + 1)
    offsets = (np.arange(PATTERNS) + 0.5) / PATTERNS - 0.5
    spread = shifts[:, None] - offsets[None, :]
    table = np.zeros((8, LANES), np.float32)
    table[: 2 * RADIUS + 1, :PATTERNS] = (
        np.sinc(spread) * np.cos(np.pi * spread / (2 * RADIUS + 2)) ** 2
    )
    return table


def dft_table(length):
    times = np.arange(length // 2)
    freqs = np.arange(length // 2)
    phase = 2.0 * np.pi * (freqs[:, None] * times[None, :] % length) / length
    full = np.concatenate([np.cos(phase), -np.sin(phase)], axis=0) / math.sqrt(length)
    full = full.reshape(NX, -1, 2, length // 2).transpose(0, 2, 1, 3)
    high = full.astype(jnp.bfloat16)
    low = (full - high.astype(np.float64)).astype(jnp.bfloat16)
    return np.concatenate([high, low], axis=2)


def split(values):
    high = values.astype(jnp.bfloat16)
    return high, (values - high.astype(jnp.float32)).astype(jnp.bfloat16)


def dot_nt(a, b):
    return lax.dot_general(a, b, NT_DOT, preferred_element_type=jnp.float32)


def place():
    b = lax.axis_index("bin")
    return b // (NZ * NC), b // NC % NZ, b % NC, lax.axis_index("line")


def device(x, z, c):
    return (x * NZ + z) * NC + c


X_ORDER = (0, 2, 1, 3)
OWN = NZ * NC - NC


def offsets(k):
    i, d, e = k // (NZ * NC), k // NC % NZ, k % NC
    along_x = jnp.where(i == 1, X_ORDER[1], jnp.where(i == 2, X_ORDER[2], i))
    along_z = NZ // 2 + jnp.where(d % 2 == 1, -((d + 1) // 2), d // 2)
    return along_x, along_z, e


def unit_of(k):
    late = k - (N_BIN - 2 * LAST)
    return jnp.where(late < 0, k // GROUP, (N_BIN - 2 * LAST) // GROUP + late // LAST)


def wait_for(ref, sem):
    pltpu.make_async_copy(ref, ref, sem).wait()


def kernel(
    traces_hbm, cell_hbm, pattern_hbm, fold_hbm, table_hbm, sinc_hbm,
    out_ref,
    traces, cells, patterns, own_fold, table, sinc, spec, recv, meta, folds, fold_sum, acc, onehot, mixed, halo,
    load_sem, entered, meta_sem, fold_sem, send_sem, recv_sem, halo_sem,
):
    bins = acc.shape[1]
    x, z, c, y = place()
    me = device(x, z, c)
    above, below = (y + 1) % NY, (y + NY - 1) % NY
    columns = NX * NC

    def along_z(k):
        return device(x, (z + k) % NZ, c), y

    def across(k):
        return device((x + k // NC) % NX, z, (c + k) % NC), y

    def copies(ref, slots, peer, sem):
        for k in range(1, slots):
            pltpu.make_async_remote_copy(
                ref.at[0], ref.at[k], sem.at[0], sem.at[1],
                device_id=peer(k), device_id_type=MESH).start()

    barrier = pltpu.get_barrier_semaphore()
    neighbours = [along_z(k) for k in range(1, NZ)] + [across(k) for k in range(1, columns)]
    for other in neighbours:
        pl.semaphore_signal(barrier, inc=1, device_id=other, device_id_type=MESH)

    @pl.when(y > 0)
    def _():
        pl.semaphore_signal(barrier, inc=1, device_id=(me, below), device_id_type=MESH)

    @pl.when(y < NY - 1)
    def _():
        pl.semaphore_signal(barrier, inc=1, device_id=(me, above), device_id_type=MESH)

    pairs = [(cell_hbm, cells), (pattern_hbm, patterns), (fold_hbm, own_fold), (traces_hbm, traces)]
    pairs += [(table_hbm.at[(x + i) % NX], table.at[n]) for n, i in enumerate(X_ORDER)]
    pairs += [(sinc_hbm, sinc)]
    loads = [
        pltpu.make_async_copy(source, target, load_sem.at[i])
        for i, (source, target) in enumerate(pairs)
    ]
    for load in loads:
        load.start()

    both_sides = jnp.where((y > 0) & (y < NY - 1), 2, 1)
    pl.semaphore_wait(barrier, len(neighbours) + both_sides)
    for k in range(1, columns):
        pl.semaphore_signal(entered, inc=1, device_id=across(k), device_id_type=MESH)

    loads[0].wait()
    loads[1].wait()
    for i in range(2):
        meta[0, 0, pl.ds(i, 1), :] = cells[:, pl.ds(i * LANES, LANES)]
        meta[0, 0, pl.ds(2 + i, 1), :] = patterns[:, pl.ds(i * LANES, LANES)]
    copies(meta.at[0], NZ, along_z, meta_sem.at[0])
    loads[2].wait()
    lanes = own_fold.shape[1]
    spread_row = lax.broadcasted_iota(jnp.int32, (lanes, LANES), 0)
    spread_lane = lax.broadcasted_iota(jnp.int32, (lanes, LANES), 1)
    spread = (spread_lane == (z % 4) * (NC * lanes) + c * lanes + spread_row).astype(jnp.float32)
    fold_row = jnp.dot(
        own_fold[...].astype(jnp.float32), spread, preferred_element_type=jnp.float32
    )
    fold_both = jnp.concatenate([fold_row, fold_row], axis=0)
    half = lax.broadcasted_iota(jnp.int32, fold_both.shape, 0) // 4
    folds[0] = jnp.where(half == z // 4, fold_both, 0.0)
    copies(folds, NZ, along_z, fold_sem.at[0])

    loads[3].wait()
    middle = traces.shape[1] // 2
    early, late = traces[:, :middle], traces[:, middle:]
    parts = [split(early + late), split(early - late)]

    def transform(i):
        loads[4 + i].wait()
        for parity, (t_high, t_low) in enumerate(parts):
            both = dot_nt(table[i, parity], t_high)
            rows = both.shape[0] // 2
            value = both[:rows] + both[rows:] + dot_nt(table[i, parity, :rows], t_low)
            at = pl.ds((x + X_ORDER[i]) % NX * (NZ * NC), NZ * NC)
            spec[at, parity] = value.reshape(NZ * NC, rows // (NZ * NC), -1)

    def start(k):
        i, d, e = offsets(k)
        target = device((x + i) % NX, (z + d) % NZ, (c + e) % NC)
        pltpu.make_async_remote_copy(
            spec.at[target], recv.at[k], send_sem.at[0], recv_sem.at[unit_of(k)],
            device_id=(target, y), device_id_type=MESH).start()

    def start_one(k, carry):
        start(k)
        return carry

    transform(0)
    for d in range(NZ - 1):
        start(d * NC)
    pltpu.make_async_copy(spec.at[me], recv.at[OWN], recv_sem.at[unit_of(OWN)]).start()
    pl.semaphore_wait(entered, columns - 1)
    for d in range(NZ):
        start(d * NC + 1)
    wait_for(meta.at[0, pl.ds(1, NZ - 1)], meta_sem.at[0, 1])
    copies(meta, columns, across, meta_sem.at[1])
    wait_for(folds.at[pl.ds(1, NZ - 1)], fold_sem.at[0, 1])
    fold_sum[0] = jnp.sum(folds[...], axis=0)
    copies(fold_sum, columns, across, fold_sem.at[1])
    for i in range(1, NX):
        transform(i)
        lax.fori_loop(i * NZ * NC, (i + 1) * NZ * NC, start_one, 0)

    loads[-1].wait()
    acc[...] = jnp.zeros_like(acc)
    wait_for(meta.at[pl.ds(1, columns - 1)], meta_sem.at[1, 1])

    slice_rows = recv.shape[1] * recv.shape[2]
    records = recv.shape[3]
    full = 8 * slice_rows

    def tags_of(k):
        i, d, e = offsets(k)
        tags = meta[i * NC + e, d]
        return (
            jnp.concatenate([tags[0:1], tags[1:2]], axis=1),
            jnp.concatenate([tags[2:3], tags[3:4]], axis=1),
        )

    def weigh(cell, pattern):
        pattern = jnp.broadcast_to(pattern, (8, records))
        taps = jnp.zeros((8, records), jnp.float32)
        for q in range(PATTERNS):
            taps = jnp.where(pattern == q, sinc[:, q : q + 1], taps)
        line = jnp.broadcast_to(cell // bins, (8, records))
        weights = taps
        for s in range(1, 4):
            weights = jnp.where(line == s, pltpu.roll(taps, s, 0), weights)
        return jnp.concatenate([weights[0:2], weights[6:8], weights[2:6]], axis=0)

    def mark(j, cell):
        where = cell % bins
        for g in range(0, bins, 256):
            row = lax.broadcasted_iota(jnp.int32, (256, records), 0) + g
            onehot[pl.ds(g, 256), pl.ds(j * records, records)] = (
                (row == jnp.broadcast_to(where, (256, records)))
                .astype(jnp.float32)
                .astype(jnp.bfloat16)
            )

    def mix(k, j, weights):
        block = recv[k].reshape(slice_rows, records)
        terms = (weights[:, None, :] * block[None, :, :]).reshape(full, records)
        t_high, t_low = split(terms)
        at = pl.ds(j * records, records)
        edge = full // 2
        mixed[pl.ds(0, edge), at] = t_high[:edge]
        mixed[pl.ds(edge, edge), at] = t_low[:edge]
        mixed[pl.ds(2 * edge, edge), at] = t_high[edge:]
        mixed[pl.ds(3 * edge, edge), at] = t_low[edge:]

    def add(rows, count, first=0, end=bins):
        depth = pl.ds(0, count * records)
        for g in range(first, end, 256):
            acc[rows, pl.ds(g, 256)] += dot_nt(mixed[rows, depth], onehot[pl.ds(g, 256), depth])

    def stack(i, carry):
        wait_for(recv.at[pl.ds(i * GROUP, GROUP)], recv_sem.at[i])
        for j in range(GROUP):
            k = i * GROUP + j
            cell, pattern = tags_of(k)
            mix(k, j, weigh(cell, pattern))
            mark(j, cell)
        add(pl.ds(0, 2 * full), GROUP)
        return carry

    whole = (N_BIN - 2 * LAST) // GROUP
    lax.fori_loop(0, whole, stack, 0)

    def prepare(at):
        weights = []
        for j in range(LAST):
            cell, pattern = tags_of(at + j)
            weights.append(weigh(cell, pattern))
            mark(j, cell)
        return weights

    weights = prepare(N_BIN - 2 * LAST)
    wait_for(recv.at[pl.ds(N_BIN - 2 * LAST, LAST)], recv_sem.at[whole])
    for j in range(LAST):
        mix(N_BIN - 2 * LAST + j, j, weights[j])
    add(pl.ds(0, 2 * full), LAST)
    weights = prepare(N_BIN - LAST)
    wait_for(fold_sum.at[pl.ds(1, columns - 1)], fold_sem.at[1, 1])
    counts = []
    for i in range(NX):
        slot = (x + NX - i) % NX * NC
        counts.append(fold_sum[slot] + fold_sum[slot + 1])
    inverse = 1.0 / jnp.concatenate(
        [block[4 * h : 4 * h + 4] for block in counts for h in range(2)], axis=1
    )
    wait_for(recv.at[pl.ds(N_BIN - LAST, LAST)], recv_sem.at[whole + 1])
    for j in range(LAST):
        mix(N_BIN - LAST + j, j, weights[j])
    edge = 2 * slice_rows
    part = bins // 2
    swaps = []
    for p in range(2):
        at = pl.ds(p * part, part)
        add(pl.ds(0, full), LAST, p * part, (p + 1) * part)
        for i in range(2):
            halo[p, i] = acc[pl.ds(i * edge, edge), at] + acc[pl.ds((2 + i) * edge, edge), at]
        down, up = [
            pltpu.make_async_remote_copy(
                halo.at[p, i], halo.at[p, 2 + i], halo_sem.at[p, i], halo_sem.at[p, 2 + i],
                device_id=(me, other), device_id_type=MESH)
            for i, other in enumerate((below, above))
        ]
        pl.when(y > 0)(down.start)
        pl.when(y < NY - 1)(up.start)
        swaps.append((down, up))
    add(pl.ds(full, full), LAST)
    wait_for(meta.at[0, pl.ds(1, NZ - 1)], meta_sem.at[0, 0])
    wait_for(meta.at[pl.ds(1, columns - 1)], meta_sem.at[1, 0])
    wait_for(folds.at[pl.ds(1, NZ - 1)], fold_sem.at[0, 0])
    wait_for(fold_sum.at[pl.ds(1, columns - 1)], fold_sem.at[1, 0])
    wait_for(recv.at[pl.ds(1, N_BIN - 1)], send_sem.at[0])
    for p, (down, up) in enumerate(swaps):

        @pl.when(y > 0)
        def _():
            down.wait_send()
            up.wait_recv()

        @pl.when(y < NY - 1)
        def _():
            up.wait_send()
            down.wait_recv()

        at = pl.ds(p * part, part)
        for line in range(4):
            rows = full + line * slice_rows
            value = acc[pl.ds(rows, slice_rows), at] + acc[pl.ds(rows + full // 2, slice_rows), at]
            if line < 2:
                extra = halo[p, 3, pl.ds(line * slice_rows, slice_rows), :]
                inside = y > 0
            else:
                extra = halo[p, 2, pl.ds((line - 2) * slice_rows, slice_rows), :]
                inside = y < NY - 1
            scale = inverse[line : line + 1, p * part : (p + 1) * part]
            value = (value + jnp.where(inside, extra, 0.0)) * scale
            for parity in range(2):
                out_ref[:, parity, line, at] = value[parity * 8 : parity * 8 + 8]


def per_device(traces, trace_cell, pattern, fold):
    _, records, length = traces.shape
    lines, bins_dev = fold.shape
    bins = bins_dev * N_BIN
    rows = length // N_BIN
    table = dft_table(length)
    anywhere = pl.BlockSpec(memory_space=pl.ANY)
    f32, i32, bf16 = jnp.float32, jnp.int32, jnp.bfloat16
    dma = pltpu.SemaphoreType.DMA
    out = pl.pallas_call(
        kernel,
        out_shape=jax.ShapeDtypeStruct((rows // 2, 2, lines, bins), f32),
        in_specs=[anywhere] * 6,
        out_specs=pl.BlockSpec(memory_space=pltpu.VMEM),
        scratch_shapes=[
            pltpu.VMEM((records, length), f32),
            pltpu.VMEM((1, records), i32),
            pltpu.VMEM((1, records), i32),
            pltpu.VMEM((lines, bins_dev), i32),
            pltpu.VMEM(table.shape, bf16),
            pltpu.VMEM((8, LANES), f32),
            pltpu.VMEM((N_BIN, 2, rows // 2, records), f32),
            pltpu.VMEM((N_BIN, 2, rows // 2, records), f32),
            pltpu.VMEM((NX * NC, NZ, 4, LANES), i32),
            pltpu.VMEM((NZ, 8, LANES), f32),
            pltpu.VMEM((NX * NC, 8, LANES), f32),
            pltpu.VMEM((16 * rows, bins), f32),
            pltpu.VMEM((bins, GROUP * records), bf16),
            pltpu.VMEM((16 * rows, GROUP * records), bf16),
            pltpu.VMEM((2, 4, 2 * rows, bins // 2), f32),
            dma((5 + NX,)),
            pltpu.SemaphoreType.REGULAR,
            dma((2, 2)),
            dma((2, 2)),
            dma((1,)),
            dma((N_BIN // GROUP + 1,)),
            dma((2, 4)),
        ],
        compiler_params=pltpu.CompilerParams(
            collective_id=0, has_side_effects=True, vmem_limit_bytes=63 << 20
        ),
    )(traces[0], trace_cell, pattern, fold, jnp.asarray(table), jnp.asarray(sinc_table()))
    return out.reshape(rows, lines, bins)


def solution(mesh):
    return jax.shard_map(
        per_device,
        mesh=mesh,
        in_specs=(P("line", "bin", None), P("line", "bin"), P("line", "bin"), P("line", "bin")),
        out_specs=P("bin", "line", None),
        check_vma=False,
    )
```

```python
import functools
import math

import jax
import jax.numpy as jnp
import numpy as np
from jax import lax
from jax.experimental import pallas as pl
from jax.experimental.pallas import tpu as pltpu
from jax.sharding import PartitionSpec as P

RADIUS = 2
PATTERNS = 16
NX, NZ, NC, NY = 4, 8, 2, 4
N_BIN = NX * NZ * NC
LANES = 128
GROUP = 8
LAST = 4
NT_DOT = (((1,), (1,)), ((), ()))
MESH = pl.DeviceIdType.MESH


def sinc_table():
    shifts = np.arange(-RADIUS, RADIUS + 1)
    offsets = (np.arange(PATTERNS) + 0.5) / PATTERNS - 0.5
    spread = shifts[:, None] - offsets[None, :]
    table = np.zeros((8, LANES), np.float32)
    table[: 2 * RADIUS + 1, :PATTERNS] = (
        np.sinc(spread) * np.cos(np.pi * spread / (2 * RADIUS + 2)) ** 2
    )
    return table


def dft_table(length):
    times = np.arange(length // 2)
    freqs = np.arange(length // 2)
    phase = 2.0 * np.pi * (freqs[:, None] * times[None, :] % length) / length
    full = np.concatenate([np.cos(phase), -np.sin(phase)], axis=0) / math.sqrt(length)
    full = full.reshape(NX, -1, 2, length // 2).transpose(0, 2, 1, 3)
    high = full.astype(jnp.bfloat16)
    low = (full - high.astype(np.float64)).astype(jnp.bfloat16)
    return np.concatenate([high, low], axis=2)


def split(values):
    high = values.astype(jnp.bfloat16)
    return high, (values - high.astype(jnp.float32)).astype(jnp.bfloat16)


def dot_nt(a, b):
    return lax.dot_general(a, b, NT_DOT, preferred_element_type=jnp.float32)


def place():
    b = lax.axis_index("bin")
    return b // (NZ * NC), b // NC % NZ, b % NC, lax.axis_index("line")


def device(x, z, c):
    return (x * NZ + z) * NC + c


X_ORDER = (0, 2, 1, 3)
OWN = 0


def offsets(k):
    i, d, e = k // (NZ * NC), k // NC % NZ, k % NC
    along_x = jnp.where(i == 1, X_ORDER[1], jnp.where(i == 2, X_ORDER[2], i))
    along_z = jnp.where(d % 2 == 1, (d + 1) // 2, (NZ - d // 2) % NZ)
    return along_x, along_z, e


def unit_of(k):
    late = k - (N_BIN - 2 * LAST)
    return jnp.where(late < 0, k // GROUP, (N_BIN - 2 * LAST) // GROUP + late // LAST)


def wait_for(ref, sem):
    pltpu.make_async_copy(ref, ref, sem).wait()


def kernel(
    traces_hbm, cell_hbm, pattern_hbm, fold_hbm, table_hbm, sinc_hbm,
    out_ref,
    traces, cells, patterns, own_fold, table, sinc, spec, recv, meta, folds, fold_sum, acc, onehot, mixed, halo,
    load_sem, entered, meta_sem, fold_sem, send_sem, recv_sem, halo_sem,
):
    bins = acc.shape[1]
    x, z, c, y = place()
    me = device(x, z, c)
    above, below = (y + 1) % NY, (y + NY - 1) % NY
    columns = NX * NC

    def along_z(k):
        return device(x, (z + k) % NZ, c), y

    def across(k):
        return device((x + k // NC) % NX, z, (c + k) % NC), y

    def copies(ref, slots, peer, sem):
        for k in range(1, slots):
            pltpu.make_async_remote_copy(
                ref.at[0], ref.at[k], sem.at[0], sem.at[1],
                device_id=peer(k), device_id_type=MESH).start()

    barrier = pltpu.get_barrier_semaphore()
    neighbours = [along_z(k) for k in range(1, NZ)] + [across(k) for k in range(1, columns)]
    for other in neighbours:
        pl.semaphore_signal(barrier, inc=1, device_id=other, device_id_type=MESH)

    @pl.when(y > 0)
    def _():
        pl.semaphore_signal(barrier, inc=1, device_id=(me, below), device_id_type=MESH)

    @pl.when(y < NY - 1)
    def _():
        pl.semaphore_signal(barrier, inc=1, device_id=(me, above), device_id_type=MESH)

    pairs = [(cell_hbm, cells), (pattern_hbm, patterns), (fold_hbm, own_fold), (traces_hbm, traces)]
    pairs += [(table_hbm.at[(x + i) % NX], table.at[n]) for n, i in enumerate(X_ORDER)]
    pairs += [(sinc_hbm, sinc)]
    loads = [
        pltpu.make_async_copy(source, target, load_sem.at[i])
        for i, (source, target) in enumerate(pairs)
    ]
    for load in loads:
        load.start()

    both_sides = jnp.where((y > 0) & (y < NY - 1), 2, 1)
    pl.semaphore_wait(barrier, len(neighbours) + both_sides)
    for k in range(1, columns):
        pl.semaphore_signal(entered, inc=1, device_id=across(k), device_id_type=MESH)

    loads[0].wait()
    loads[1].wait()
    for i in range(2):
        meta[0, 0, pl.ds(i, 1), :] = cells[:, pl.ds(i * LANES, LANES)]
        meta[0, 0, pl.ds(2 + i, 1), :] = patterns[:, pl.ds(i * LANES, LANES)]
    copies(meta.at[0], NZ, along_z, meta_sem.at[0])
    loads[2].wait()
    lanes = own_fold.shape[1]
    spread_row = lax.broadcasted_iota(jnp.int32, (lanes, LANES), 0)
    spread_lane = lax.broadcasted_iota(jnp.int32, (lanes, LANES), 1)
    spread = (spread_lane == (z % 4) * (NC * lanes) + c * lanes + spread_row).astype(jnp.float32)
    fold_row = jnp.dot(
        own_fold[...].astype(jnp.float32), spread, preferred_element_type=jnp.float32
    )
    fold_both = jnp.concatenate([fold_row, fold_row], axis=0)
    half = lax.broadcasted_iota(jnp.int32, fold_both.shape, 0) // 4
    folds[0] = jnp.where(half == z // 4, fold_both, 0.0)
    copies(folds, NZ, along_z, fold_sem.at[0])

    loads[3].wait()
    middle = traces.shape[1] // 2
    early, late = traces[:, :middle], traces[:, middle:]
    parts = [split(early + late), split(early - late)]

    def transform(i):
        loads[4 + i].wait()
        for parity, (t_high, t_low) in enumerate(parts):
            both = dot_nt(table[i, parity], t_high)
            rows = both.shape[0] // 2
            value = both[:rows] + both[rows:] + dot_nt(table[i, parity, :rows], t_low)
            at = pl.ds((x + X_ORDER[i]) % NX * (NZ * NC), NZ * NC)
            spec[at, parity] = value.reshape(NZ * NC, rows // (NZ * NC), -1)

    def start(k):
        i, d, e = offsets(k)
        target = device((x + i) % NX, (z + d) % NZ, (c + e) % NC)
        pltpu.make_async_remote_copy(
            spec.at[target], recv.at[k], send_sem.at[0], recv_sem.at[unit_of(k)],
            device_id=(target, y), device_id_type=MESH).start()

    def start_one(k, carry):
        start(k)
        return carry

    transform(0)
    for d in range(1, NZ):
        start(d * NC)
    pltpu.make_async_copy(spec.at[me], recv.at[OWN], recv_sem.at[unit_of(OWN)]).start()
    pl.semaphore_wait(entered, columns - 1)
    for d in range(NZ):
        start(d * NC + 1)
    wait_for(meta.at[0, pl.ds(1, NZ - 1)], meta_sem.at[0, 1])
    copies(meta, columns, across, meta_sem.at[1])
    wait_for(folds.at[pl.ds(1, NZ - 1)], fold_sem.at[0, 1])
    fold_sum[0] = jnp.sum(folds[...], axis=0)
    copies(fold_sum, columns, across, fold_sem.at[1])
    for i in range(1, NX):
        transform(i)
        lax.fori_loop(i * NZ * NC, (i + 1) * NZ * NC, start_one, 0)

    loads[-1].wait()
    acc[...] = jnp.zeros_like(acc)
    wait_for(meta.at[pl.ds(1, columns - 1)], meta_sem.at[1, 1])

    slice_rows = recv.shape[1] * recv.shape[2]
    records = recv.shape[3]
    full = 8 * slice_rows

    def tags_of(k):
        i, d, e = offsets(k)
        tags = meta[i * NC + e, d]
        return (
            jnp.concatenate([tags[0:1], tags[1:2]], axis=1),
            jnp.concatenate([tags[2:3], tags[3:4]], axis=1),
        )

    def weigh(cell, pattern):
        pattern = jnp.broadcast_to(pattern, (8, records))
        taps = jnp.zeros((8, records), jnp.float32)
        for q in range(PATTERNS):
            taps = jnp.where(pattern == q, sinc[:, q : q + 1], taps)
        line = jnp.broadcast_to(cell // bins, (8, records))
        weights = taps
        for s in range(1, 4):
            weights = jnp.where(line == s, pltpu.roll(taps, s, 0), weights)
        return jnp.concatenate([weights[0:2], weights[6:8], weights[2:6]], axis=0)

    def mark(j, cell):
        where = cell % bins
        for g in range(0, bins, 256):
            row = lax.broadcasted_iota(jnp.int32, (256, records), 0) + g
            onehot[pl.ds(g, 256), pl.ds(j * records, records)] = (
                (row == jnp.broadcast_to(where, (256, records)))
                .astype(jnp.float32)
                .astype(jnp.bfloat16)
            )

    def mix(k, j, weights):
        block = recv[k].reshape(slice_rows, records)
        terms = (weights[:, None, :] * block[None, :, :]).reshape(full, records)
        t_high, t_low = split(terms)
        at = pl.ds(j * records, records)
        edge = full // 2
        mixed[pl.ds(0, edge), at] = t_high[:edge]
        mixed[pl.ds(edge, edge), at] = t_low[:edge]
        mixed[pl.ds(2 * edge, edge), at] = t_high[edge:]
        mixed[pl.ds(3 * edge, edge), at] = t_low[edge:]

    def add(rows, count, first=0, end=bins):
        depth = pl.ds(0, count * records)
        for g in range(first, end, 256):
            acc[rows, pl.ds(g, 256)] += dot_nt(mixed[rows, depth], onehot[pl.ds(g, 256), depth])

    def stack(i, carry):
        wait_for(recv.at[pl.ds(i * GROUP, GROUP)], recv_sem.at[i])
        for j in range(GROUP):
            k = i * GROUP + j
            cell, pattern = tags_of(k)
            mix(k, j, weigh(cell, pattern))
            mark(j, cell)
        add(pl.ds(0, 2 * full), GROUP)
        return carry

    whole = (N_BIN - 2 * LAST) // GROUP
    lax.fori_loop(0, whole, stack, 0)

    def prepare(at):
        weights = []
        for j in range(LAST):
            cell, pattern = tags_of(at + j)
            weights.append(weigh(cell, pattern))
            mark(j, cell)
        return weights

    weights = prepare(N_BIN - 2 * LAST)
    wait_for(recv.at[pl.ds(N_BIN - 2 * LAST, LAST)], recv_sem.at[whole])
    for j in range(LAST):
        mix(N_BIN - 2 * LAST + j, j, weights[j])
    add(pl.ds(0, 2 * full), LAST)
    weights = prepare(N_BIN - LAST)
    wait_for(fold_sum.at[pl.ds(1, columns - 1)], fold_sem.at[1, 1])
    counts = []
    for i in range(NX):
        slot = (x + NX - i) % NX * NC
        counts.append(fold_sum[slot] + fold_sum[slot + 1])
    inverse = 1.0 / jnp.concatenate(
        [block[4 * h : 4 * h + 4] for block in counts for h in range(2)], axis=1
    )
    wait_for(recv.at[pl.ds(N_BIN - LAST, LAST)], recv_sem.at[whole + 1])
    for j in range(LAST):
        mix(N_BIN - LAST + j, j, weights[j])
    edge = 2 * slice_rows
    part = bins // 2
    swaps = []
    for p in range(2):
        at = pl.ds(p * part, part)
        add(pl.ds(0, full), LAST, p * part, (p + 1) * part)
        for i in range(2):
            halo[p, i] = acc[pl.ds(i * edge, edge), at] + acc[pl.ds((2 + i) * edge, edge), at]
        down, up = [
            pltpu.make_async_remote_copy(
                halo.at[p, i], halo.at[p, 2 + i], halo_sem.at[p, i], halo_sem.at[p, 2 + i],
                device_id=(me, other), device_id_type=MESH)
            for i, other in enumerate((below, above))
        ]
        pl.when(y > 0)(down.start)
        pl.when(y < NY - 1)(up.start)
        swaps.append((down, up))
    add(pl.ds(full, full), LAST)
    wait_for(meta.at[0, pl.ds(1, NZ - 1)], meta_sem.at[0, 0])
    wait_for(meta.at[pl.ds(1, columns - 1)], meta_sem.at[1, 0])
    wait_for(folds.at[pl.ds(1, NZ - 1)], fold_sem.at[0, 0])
    wait_for(fold_sum.at[pl.ds(1, columns - 1)], fold_sem.at[1, 0])
    wait_for(recv.at[pl.ds(1, N_BIN - 1)], send_sem.at[0])
    for p, (down, up) in enumerate(swaps):

        @pl.when(y > 0)
        def _():
            down.wait_send()
            up.wait_recv()

        @pl.when(y < NY - 1)
        def _():
            up.wait_send()
            down.wait_recv()

        at = pl.ds(p * part, part)
        for line in range(4):
            rows = full + line * slice_rows
            value = acc[pl.ds(rows, slice_rows), at] + acc[pl.ds(rows + full // 2, slice_rows), at]
            if line < 2:
                extra = halo[p, 3, pl.ds(line * slice_rows, slice_rows), :]
                inside = y > 0
            else:
                extra = halo[p, 2, pl.ds((line - 2) * slice_rows, slice_rows), :]
                inside = y < NY - 1
            scale = inverse[line : line + 1, p * part : (p + 1) * part]
            value = (value + jnp.where(inside, extra, 0.0)) * scale
            for parity in range(2):
                out_ref[:, parity, line, at] = value[parity * 8 : parity * 8 + 8]


def per_device(traces, trace_cell, pattern, fold):
    _, records, length = traces.shape
    lines, bins_dev = fold.shape
    bins = bins_dev * N_BIN
    rows = length // N_BIN
    table = dft_table(length)
    anywhere = pl.BlockSpec(memory_space=pl.ANY)
    f32, i32, bf16 = jnp.float32, jnp.int32, jnp.bfloat16
    dma = pltpu.SemaphoreType.DMA
    out = pl.pallas_call(
        kernel,
        out_shape=jax.ShapeDtypeStruct((rows // 2, 2, lines, bins), f32),
        in_specs=[anywhere] * 6,
        out_specs=pl.BlockSpec(memory_space=pltpu.VMEM),
        scratch_shapes=[
            pltpu.VMEM((records, length), f32),
            pltpu.VMEM((1, records), i32),
            pltpu.VMEM((1, records), i32),
            pltpu.VMEM((lines, bins_dev), i32),
            pltpu.VMEM(table.shape, bf16),
            pltpu.VMEM((8, LANES), f32),
            pltpu.VMEM((N_BIN, 2, rows // 2, records), f32),
            pltpu.VMEM((N_BIN, 2, rows // 2, records), f32),
            pltpu.VMEM((NX * NC, NZ, 4, LANES), i32),
            pltpu.VMEM((NZ, 8, LANES), f32),
            pltpu.VMEM((NX * NC, 8, LANES), f32),
            pltpu.VMEM((16 * rows, bins), f32),
            pltpu.VMEM((bins, GROUP * records), bf16),
            pltpu.VMEM((16 * rows, GROUP * records), bf16),
            pltpu.VMEM((2, 4, 2 * rows, bins // 2), f32),
            dma((5 + NX,)),
            pltpu.SemaphoreType.REGULAR,
            dma((2, 2)),
            dma((2, 2)),
            dma((1,)),
            dma((N_BIN // GROUP + 1,)),
            dma((2, 4)),
        ],
        compiler_params=pltpu.CompilerParams(
            collective_id=0, has_side_effects=True, vmem_limit_bytes=63 << 20
        ),
    )(traces[0], trace_cell, pattern, fold, jnp.asarray(table), jnp.asarray(sinc_table()))
    return out.reshape(rows, lines, bins)


def solution(mesh):
    return jax.shard_map(
        per_device,
        mesh=mesh,
        in_specs=(P("line", "bin", None), P("line", "bin"), P("line", "bin"), P("line", "bin")),
        out_specs=P("bin", "line", None),
        check_vma=False,
    )
```

```python
import functools
import math

import jax
import jax.numpy as jnp
import numpy as np
from jax import lax
from jax.experimental import pallas as pl
from jax.experimental.pallas import tpu as pltpu
from jax.sharding import PartitionSpec as P

RADIUS = 2
PATTERNS = 16
NX, NZ, NC, NY = 4, 8, 2, 4
N_BIN = NX * NZ * NC
LANES = 128
GROUP = 8
LAST = 4
NT_DOT = (((1,), (1,)), ((), ()))
MESH = pl.DeviceIdType.MESH


def sinc_table():
    shifts = np.arange(-RADIUS, RADIUS + 1)
    offsets = (np.arange(PATTERNS) + 0.5) / PATTERNS - 0.5
    spread = shifts[:, None] - offsets[None, :]
    table = np.zeros((8, LANES), np.float32)
    table[: 2 * RADIUS + 1, :PATTERNS] = (
        np.sinc(spread) * np.cos(np.pi * spread / (2 * RADIUS + 2)) ** 2
    )
    return table


def dft_table(length):
    times = np.arange(length // 2)
    freqs = np.arange(length // 2)
    phase = 2.0 * np.pi * (freqs[:, None] * times[None, :] % length) / length
    full = np.concatenate([np.cos(phase), -np.sin(phase)], axis=0) / math.sqrt(length)
    full = full.reshape(NX, -1, 2, length // 2).transpose(0, 2, 1, 3)
    high = full.astype(jnp.bfloat16)
    low = (full - high.astype(np.float64)).astype(jnp.bfloat16)
    return np.concatenate([high, low], axis=2)


def split(values):
    high = values.astype(jnp.bfloat16)
    return high, (values - high.astype(jnp.float32)).astype(jnp.bfloat16)


def dot_nt(a, b):
    return lax.dot_general(a, b, NT_DOT, preferred_element_type=jnp.float32)


def place():
    b = lax.axis_index("bin")
    return b // (NZ * NC), b // NC % NZ, b % NC, lax.axis_index("line")


def device(x, z, c):
    return (x * NZ + z) * NC + c


X_ORDER = (0, 2, 1, 3)
OWN = 0


def offsets(k):
    i, d, e = k // (NZ * NC), k // NC % NZ, k % NC
    along_x = jnp.where(i == 1, X_ORDER[1], jnp.where(i == 2, X_ORDER[2], i))
    along_z = jnp.where(d % 2 == 1, (d + 1) // 2, (NZ - d // 2) % NZ)
    return along_x, along_z, e


def unit_of(k):
    late = k - (N_BIN - 2 * LAST)
    return jnp.where(late < 0, k // GROUP, (N_BIN - 2 * LAST) // GROUP + late // LAST)


def wait_for(ref, sem):
    pltpu.make_async_copy(ref, ref, sem).wait()


def kernel(
    traces_hbm, cell_hbm, pattern_hbm, fold_hbm, table_hbm, sinc_hbm,
    out_ref,
    traces, cells, patterns, own_fold, table, sinc, spec, recv, meta, folds, fold_sum, acc, onehot, mixed, halo,
    load_sem, entered, meta_sem, fold_sem, send_sem, recv_sem, halo_sem,
):
    bins = acc.shape[1]
    x, z, c, y = place()
    me = device(x, z, c)
    above, below = (y + 1) % NY, (y + NY - 1) % NY
    columns = NX * NC

    def along_z(k):
        return device(x, (z + k) % NZ, c), y

    def across(k):
        return device((x + k // NC) % NX, z, (c + k) % NC), y

    def copies(ref, slots, peer, sem):
        for k in range(1, slots):
            pltpu.make_async_remote_copy(
                ref.at[0], ref.at[k], sem.at[0], sem.at[1],
                device_id=peer(k), device_id_type=MESH).start()

    barrier = pltpu.get_barrier_semaphore()
    neighbours = [along_z(k) for k in range(1, NZ)] + [across(k) for k in range(1, columns)]
    for other in neighbours:
        pl.semaphore_signal(barrier, inc=1, device_id=other, device_id_type=MESH)

    @pl.when(y > 0)
    def _():
        pl.semaphore_signal(barrier, inc=1, device_id=(me, below), device_id_type=MESH)

    @pl.when(y < NY - 1)
    def _():
        pl.semaphore_signal(barrier, inc=1, device_id=(me, above), device_id_type=MESH)

    pairs = [(cell_hbm, cells), (pattern_hbm, patterns), (fold_hbm, own_fold), (traces_hbm, traces)]
    pairs += [(table_hbm.at[(x + i) % NX], table.at[n]) for n, i in enumerate(X_ORDER)]
    pairs += [(sinc_hbm, sinc)]
    loads = [
        pltpu.make_async_copy(source, target, load_sem.at[i])
        for i, (source, target) in enumerate(pairs)
    ]
    for load in loads:
        load.start()

    both_sides = jnp.where((y > 0) & (y < NY - 1), 2, 1)
    pl.semaphore_wait(barrier, len(neighbours) + both_sides)
    for k in range(1, columns):
        pl.semaphore_signal(entered, inc=1, device_id=across(k), device_id_type=MESH)

    loads[0].wait()
    loads[1].wait()
    for i in range(2):
        meta[0, 0, pl.ds(i, 1), :] = cells[:, pl.ds(i * LANES, LANES)]
        meta[0, 0, pl.ds(2 + i, 1), :] = patterns[:, pl.ds(i * LANES, LANES)]
    copies(meta.at[0], NZ, along_z, meta_sem.at[0])
    loads[2].wait()
    lanes = own_fold.shape[1]
    spread_row = lax.broadcasted_iota(jnp.int32, (lanes, LANES), 0)
    spread_lane = lax.broadcasted_iota(jnp.int32, (lanes, LANES), 1)
    spread = (spread_lane == (z % 4) * (NC * lanes) + c * lanes + spread_row).astype(jnp.float32)
    fold_row = jnp.dot(
        own_fold[...].astype(jnp.float32), spread, preferred_element_type=jnp.float32
    )
    fold_both = jnp.concatenate([fold_row, fold_row], axis=0)
    half = lax.broadcasted_iota(jnp.int32, fold_both.shape, 0) // 4
    folds[0] = jnp.where(half == z // 4, fold_both, 0.0)
    copies(folds, NZ, along_z, fold_sem.at[0])

    loads[3].wait()
    middle = traces.shape[1] // 2
    early, late = traces[:, :middle], traces[:, middle:]
    parts = [split(early + late), split(early - late)]

    def transform(i):
        loads[4 + i].wait()
        for parity, (t_high, t_low) in enumerate(parts):
            both = dot_nt(table[i, parity], t_high)
            rows = both.shape[0] // 2
            value = both[:rows] + both[rows:] + dot_nt(table[i, parity, :rows], t_low)
            at = pl.ds((x + X_ORDER[i]) % NX * (NZ * NC), NZ * NC)
            spec[at, parity] = value.reshape(NZ * NC, rows // (NZ * NC), -1)

    def start(k):
        i, d, e = offsets(k)
        target = device((x + i) % NX, (z + d) % NZ, (c + e) % NC)
        pltpu.make_async_remote_copy(
            spec.at[target], recv.at[k], send_sem.at[0], recv_sem.at[unit_of(k)],
            device_id=(target, y), device_id_type=MESH).start()

    def start_one(k, carry):
        start(k)
        return carry

    transform(0)
    for d in range(1, NZ):
        start(d * NC)
    pltpu.make_async_copy(spec.at[me], recv.at[OWN], recv_sem.at[unit_of(OWN)]).start()
    pl.semaphore_wait(entered, columns - 1)
    for d in range(NZ):
        start(d * NC + 1)
    transform(1)
    lax.fori_loop(NZ * NC, 2 * NZ * NC, start_one, 0)
    wait_for(meta.at[0, pl.ds(1, NZ - 1)], meta_sem.at[0, 1])
    copies(meta, columns, across, meta_sem.at[1])
    wait_for(folds.at[pl.ds(1, NZ - 1)], fold_sem.at[0, 1])
    fold_sum[0] = jnp.sum(folds[...], axis=0)
    copies(fold_sum, columns, across, fold_sem.at[1])
    for i in range(2, NX):
        transform(i)
        lax.fori_loop(i * NZ * NC, (i + 1) * NZ * NC, start_one, 0)

    loads[-1].wait()
    acc[...] = jnp.zeros_like(acc)
    wait_for(meta.at[pl.ds(1, columns - 1)], meta_sem.at[1, 1])

    slice_rows = recv.shape[1] * recv.shape[2]
    records = recv.shape[3]
    full = 8 * slice_rows

    def tags_of(k):
        i, d, e = offsets(k)
        tags = meta[i * NC + e, d]
        return (
            jnp.concatenate([tags[0:1], tags[1:2]], axis=1),
            jnp.concatenate([tags[2:3], tags[3:4]], axis=1),
        )

    def weigh(cell, pattern):
        pattern = jnp.broadcast_to(pattern, (8, records))
        taps = jnp.zeros((8, records), jnp.float32)
        for q in range(PATTERNS):
            taps = jnp.where(pattern == q, sinc[:, q : q + 1], taps)
        line = jnp.broadcast_to(cell // bins, (8, records))
        weights = taps
        for s in range(1, 4):
            weights = jnp.where(line == s, pltpu.roll(taps, s, 0), weights)
        return jnp.concatenate([weights[0:2], weights[6:8], weights[2:6]], axis=0)

    def mark(j, cell):
        where = cell % bins
        for g in range(0, bins, 256):
            row = lax.broadcasted_iota(jnp.int32, (256, records), 0) + g
            onehot[pl.ds(g, 256), pl.ds(j * records, records)] = (
                (row == jnp.broadcast_to(where, (256, records)))
                .astype(jnp.float32)
                .astype(jnp.bfloat16)
            )

    def mix(k, j, weights):
        block = recv[k].reshape(slice_rows, records)
        terms = (weights[:, None, :] * block[None, :, :]).reshape(full, records)
        t_high, t_low = split(terms)
        at = pl.ds(j * records, records)
        edge = full // 2
        mixed[pl.ds(0, edge), at] = t_high[:edge]
        mixed[pl.ds(edge, edge), at] = t_low[:edge]
        mixed[pl.ds(2 * edge, edge), at] = t_high[edge:]
        mixed[pl.ds(3 * edge, edge), at] = t_low[edge:]

    def add(rows, count, first=0, end=bins):
        depth = pl.ds(0, count * records)
        for g in range(first, end, 256):
            acc[rows, pl.ds(g, 256)] += dot_nt(mixed[rows, depth], onehot[pl.ds(g, 256), depth])

    def stack(i, carry):
        wait_for(recv.at[pl.ds(i * GROUP, GROUP)], recv_sem.at[i])
        for j in range(GROUP):
            k = i * GROUP + j
            cell, pattern = tags_of(k)
            mix(k, j, weigh(cell, pattern))
            mark(j, cell)
        add(pl.ds(0, 2 * full), GROUP)
        return carry

    whole = (N_BIN - 2 * LAST) // GROUP
    lax.fori_loop(0, whole, stack, 0)

    def prepare(at):
        weights = []
        for j in range(LAST):
            cell, pattern = tags_of(at + j)
            weights.append(weigh(cell, pattern))
            mark(j, cell)
        return weights

    weights = prepare(N_BIN - 2 * LAST)
    wait_for(recv.at[pl.ds(N_BIN - 2 * LAST, LAST)], recv_sem.at[whole])
    for j in range(LAST):
        mix(N_BIN - 2 * LAST + j, j, weights[j])
    add(pl.ds(0, 2 * full), LAST)
    weights = prepare(N_BIN - LAST)
    wait_for(fold_sum.at[pl.ds(1, columns - 1)], fold_sem.at[1, 1])
    counts = []
    for i in range(NX):
        slot = (x + NX - i) % NX * NC
        counts.append(fold_sum[slot] + fold_sum[slot + 1])
    inverse = 1.0 / jnp.concatenate(
        [block[4 * h : 4 * h + 4] for block in counts for h in range(2)], axis=1
    )
    wait_for(recv.at[pl.ds(N_BIN - LAST, LAST)], recv_sem.at[whole + 1])
    for j in range(LAST):
        mix(N_BIN - LAST + j, j, weights[j])
    edge = 2 * slice_rows
    part = bins // 2
    swaps = []
    for p in range(2):
        at = pl.ds(p * part, part)
        add(pl.ds(0, full), LAST, p * part, (p + 1) * part)
        for i in range(2):
            halo[p, i] = acc[pl.ds(i * edge, edge), at] + acc[pl.ds((2 + i) * edge, edge), at]
        down, up = [
            pltpu.make_async_remote_copy(
                halo.at[p, i], halo.at[p, 2 + i], halo_sem.at[p, i], halo_sem.at[p, 2 + i],
                device_id=(me, other), device_id_type=MESH)
            for i, other in enumerate((below, above))
        ]
        pl.when(y > 0)(down.start)
        pl.when(y < NY - 1)(up.start)
        swaps.append((down, up))
    add(pl.ds(full, full), LAST)
    wait_for(meta.at[0, pl.ds(1, NZ - 1)], meta_sem.at[0, 0])
    wait_for(meta.at[pl.ds(1, columns - 1)], meta_sem.at[1, 0])
    wait_for(folds.at[pl.ds(1, NZ - 1)], fold_sem.at[0, 0])
    wait_for(fold_sum.at[pl.ds(1, columns - 1)], fold_sem.at[1, 0])
    wait_for(recv.at[pl.ds(1, N_BIN - 1)], send_sem.at[0])
    for p, (down, up) in enumerate(swaps):

        @pl.when(y > 0)
        def _():
            down.wait_send()
            up.wait_recv()

        @pl.when(y < NY - 1)
        def _():
            up.wait_send()
            down.wait_recv()

        at = pl.ds(p * part, part)
        for line in range(4):
            rows = full + line * slice_rows
            value = acc[pl.ds(rows, slice_rows), at] + acc[pl.ds(rows + full // 2, slice_rows), at]
            if line < 2:
                extra = halo[p, 3, pl.ds(line * slice_rows, slice_rows), :]
                inside = y > 0
            else:
                extra = halo[p, 2, pl.ds((line - 2) * slice_rows, slice_rows), :]
                inside = y < NY - 1
            scale = inverse[line : line + 1, p * part : (p + 1) * part]
            value = (value + jnp.where(inside, extra, 0.0)) * scale
            for parity in range(2):
                out_ref[:, parity, line, at] = value[parity * 8 : parity * 8 + 8]


def per_device(traces, trace_cell, pattern, fold):
    _, records, length = traces.shape
    lines, bins_dev = fold.shape
    bins = bins_dev * N_BIN
    rows = length // N_BIN
    table = dft_table(length)
    anywhere = pl.BlockSpec(memory_space=pl.ANY)
    f32, i32, bf16 = jnp.float32, jnp.int32, jnp.bfloat16
    dma = pltpu.SemaphoreType.DMA
    out = pl.pallas_call(
        kernel,
        out_shape=jax.ShapeDtypeStruct((rows // 2, 2, lines, bins), f32),
        in_specs=[anywhere] * 6,
        out_specs=pl.BlockSpec(memory_space=pltpu.VMEM),
        scratch_shapes=[
            pltpu.VMEM((records, length), f32),
            pltpu.VMEM((1, records), i32),
            pltpu.VMEM((1, records), i32),
            pltpu.VMEM((lines, bins_dev), i32),
            pltpu.VMEM(table.shape, bf16),
            pltpu.VMEM((8, LANES), f32),
            pltpu.VMEM((N_BIN, 2, rows // 2, records), f32),
            pltpu.VMEM((N_BIN, 2, rows // 2, records), f32),
            pltpu.VMEM((NX * NC, NZ, 4, LANES), i32),
            pltpu.VMEM((NZ, 8, LANES), f32),
            pltpu.VMEM((NX * NC, 8, LANES), f32),
            pltpu.VMEM((16 * rows, bins), f32),
            pltpu.VMEM((bins, GROUP * records), bf16),
            pltpu.VMEM((16 * rows, GROUP * records), bf16),
            pltpu.VMEM((2, 4, 2 * rows, bins // 2), f32),
            dma((5 + NX,)),
            pltpu.SemaphoreType.REGULAR,
            dma((2, 2)),
            dma((2, 2)),
            dma((1,)),
            dma((N_BIN // GROUP + 1,)),
            dma((2, 4)),
        ],
        compiler_params=pltpu.CompilerParams(
            collective_id=0, has_side_effects=True, vmem_limit_bytes=63 << 20
        ),
    )(traces[0], trace_cell, pattern, fold, jnp.asarray(table), jnp.asarray(sinc_table()))
    return out.reshape(rows, lines, bins)


def solution(mesh):
    return jax.shard_map(
        per_device,
        mesh=mesh,
        in_specs=(P("line", "bin", None), P("line", "bin"), P("line", "bin"), P("line", "bin")),
        out_specs=P("bin", "line", None),
        check_vma=False,
    )
```
